32 devices in a mesh: groups: 2 (over y), space: 16 (over z, x, core).
Axes of the slice: x: 2, y: 2, z: 4, core: 2. Of those that a mesh axis runs over, the one named last changes fastest.
Arguments:
- image_latent: float32 [128, 16, 320], P(('groups', 'space')), parts along dimension 0, may hold values from -6 to 6
- kernel_first: float32 [3, 3, 320, 320], replicated, may hold values from -0.109375 to 0.109375
- bias_first: float32 [320], replicated, may hold values from -3 to 3
- kernel_second: float32 [3, 3, 320, 320], replicated, may hold values from -0.109375 to 0.109375
- bias_second: float32 [320], replicated, may hold values from -3 to 3
- patch_kernel: float32 [5120, 1280], P('space'), may hold values from -0.078125 to 0.078125
- patch_bias: float32 [1280], replicated, may hold values from -3 to 3
- coarse_first: float32 [3, 3, 1280, 1280], P(None, None, None, 'space'), may hold values from -0.0546875 to 0.0546875
- coarse_bias_first: float32 [1280], P('space'), may hold values from -3 to 3
- coarse_second: float32 [3, 3, 1280, 1280], P(None, None, 'space'), may hold values from -0.0546875 to 0.0546875
- coarse_bias_second: float32 [1280], replicated, may hold values from -3 to 3
Outputs:
- fine_result: float32 [128, 16, 320], P(('groups', 'space')), parts along dimension 0
- coarse_result: float32 [32, 4, 1280], P(('groups', 'space')), parts along dimension 0
The draws below stay inside these ranges and needn't reach their ends.
There are 2 independent parts, one for each index of `groups`. The reference program is written for one: setup_inputs(seed, part) draws one part's arguments, and reference() takes and returns one part's arrays. A program takes and returns all parts, laid end to end along the dimension named above; an argument that names none is the same for every part. Nothing has to cross between parts.
All inputs are finite; a program needn't handle non-finite values.
Results may differ from the reference program's by a relative error of at most 0.000061.
Values sent between devices are 32-bit elements; how exact they have to be, the bound alone decides.
A program may use at most 128 MiB of HBM per device.

```python
import jax
import jax.numpy as jnp
from jax import lax

C = 320
CC = 1280
W = 16
H = 64
HC = 16
WC = 4


def level_of(rng, shape, cuts, smallest, top_value):
    def one(axis_at, blocks):
        draws = jax.random.uniform(jax.random.fold_in(jax.random.fold_in(rng, 6), axis_at), (blocks,), jnp.float32, smallest / len(cuts), top_value / len(cuts))
        return jnp.repeat(jnp.exp(draws), shape[axis_at] // blocks).reshape((-1,) + (1,) * (len(shape) - axis_at - 1))

    factor_of = one(*cuts[0])
    for cut in cuts[1:]:
        factor_of = factor_of * one(*cut)
    return factor_of


def scatter_about(stream_key, extent, deviation, limit, cuts=(), held_as=jnp.bfloat16):
    values = jax.random.normal(stream_key, extent, jnp.float32) * deviation
    if len(cuts) > 0:
        values = level_of(stream_key, extent, cuts, -0.22, 0.18) * values
    return jnp.clip(values, min=-limit, max=limit).astype(held_as)


def setup_inputs(seed: int = 0, part: int = 0) -> dict:
    splits = jax.random.split(jax.random.key(seed), 12)
    part_splits = jax.random.split(jax.random.fold_in(splits[11], part), 12)
    image_latent = scatter_about(part_splits[0], (H, W, C), 1.0, 6.0, ((0, 16),), jnp.float32)
    kernel_first = scatter_about(splits[1], (3, 3, C, C), (9 * C) ** -0.5, 0.109375, (), jnp.float32)
    bias_first = scatter_about(splits[2], (C,), 0.5, 3.0, (), jnp.float32)
    kernel_second = scatter_about(splits[3], (3, 3, C, C), (9 * C) ** -0.5, 0.109375, (), jnp.float32)
    bias_second = scatter_about(splits[4], (C,), 0.5, 3.0, (), jnp.float32)
    patch_kernel = scatter_about(splits[5], (16 * C, CC), (16 * C) ** -0.5, 0.078125, ((0, 16),), jnp.float32)
    patch_bias = scatter_about(splits[6], (CC,), 0.5, 3.0, (), jnp.float32)
    coarse_first = scatter_about(splits[7], (3, 3, CC, CC), (9 * CC) ** -0.5, 0.0546875, ((3, 16),), jnp.float32)
    coarse_bias_first = scatter_about(splits[8], (CC,), 0.5, 3.0, ((0, 16),), jnp.float32)
    coarse_second = scatter_about(splits[9], (3, 3, CC, CC), (9 * CC) ** -0.5, 0.0546875, ((2, 16),), jnp.float32)
    coarse_bias_second = scatter_about(splits[10], (CC,), 0.5, 3.0, (), jnp.float32)
    return {"image_latent": image_latent, "kernel_first": kernel_first, "bias_first": bias_first, "kernel_second": kernel_second, "bias_second": bias_second, "patch_kernel": patch_kernel, "patch_bias": patch_bias, "coarse_first": coarse_first, "coarse_bias_first": coarse_bias_first, "coarse_second": coarse_second, "coarse_bias_second": coarse_bias_second}


def convolve(field, kernel):
    result = lax.conv_general_dilated(field[None], kernel, (1, 1), "SAME", dimension_numbers=("NHWC", "HWIO", "NHWC"), precision=lax.Precision.HIGHEST)
    return result[0]


def reference(image_latent, kernel_first, bias_first, kernel_second, bias_second, patch_kernel, patch_bias, coarse_first, coarse_bias_first, coarse_second, coarse_bias_second):
    hidden_one = convolve(jax.nn.silu(image_latent), kernel_first) + bias_first
    hidden_two = convolve(jax.nn.silu(hidden_one), kernel_second) + bias_second
    fine_result = image_latent + hidden_two
    patches = fine_result.reshape(HC, 4, WC, 4, C).transpose(0, 2, 1, 3, 4).reshape(HC * WC, 16 * C)
    product = jnp.dot(patches, patch_kernel, precision=lax.Precision.HIGHEST, preferred_element_type=jnp.float32)
    coarse_input = product.reshape(HC, WC, CC) + patch_bias
    hidden_three = convolve(jax.nn.silu(coarse_input), coarse_first) + coarse_bias_first
    hidden_four = convolve(jax.nn.silu(hidden_three), coarse_second) + coarse_bias_second
    return fine_result, coarse_input + hidden_four
```

```python
import functools

import jax
import jax.numpy as jnp
from jax import lax
from jax.experimental import pallas as pl
from jax.experimental.pallas import tpu as pltpu
from jax.sharding import PartitionSpec as P

MESH = pl.DeviceIdType.MESH
F32 = jnp.float32
BF16 = jnp.bfloat16
EDGE = 8


def split(value):
    high = value.astype(BF16)
    return high, (value - high.astype(F32)).astype(BF16)


def silu(value):
    return value / (1.0 + jnp.exp(-value))


def mul(a, b):
    return jnp.dot(a, b, preferred_element_type=F32)


def window(ref, first, rows, width, dx):
    value = ref[pl.ds(first + dx - 1, rows), :]
    if dx != 1:
        column = lax.broadcasted_iota(jnp.int32, value.shape, 0) % width
        value = jnp.where(column == (0 if dx == 0 else width - 1), 0.0, value)
    return value


def stacked(ref, first, rows, width, dx):
    high, low = split(window(ref, first, rows, width, dx))
    return jnp.concatenate([high, low], axis=0)


def kernel(
    count,
    image, bias_first, bias_second, patch_bias, coarse_bias_first, coarse_bias_second,
    w1_hbm, w2_hbm, wp_hbm, w3_hbm, w4_hbm,
    fine_out, coarse_out,
    w1, w2, wp, w3, w4,
    w1h, w1l, wph, wpl, w3s, w4h, w4l,
    halo, pad1, pad2, fine, patch_out, patch_in, sum_out, sum_in, mine, gathered, pad3, pad4, last_out, last_in,
    load_sem, halo_send, halo_recv, send_sem, recv_sem,
):
    me = lax.axis_index("space")
    rows, width, channels = image.shape
    local = mine.shape[0]
    pixels = local * count
    outer = wp.shape[1]
    feature = wp.shape[0]
    part = w3.shape[2]
    gap = w3s.shape[2] // 2

    loads = [
        pltpu.make_async_copy(src, dst, load_sem.at[i])
        for i, (src, dst) in enumerate(((w1_hbm, w1), (w2_hbm, w2), (wp_hbm, wp), (w3_hbm, w3), (w4_hbm, w4)))
    ]
    for load in loads:
        load.start()

    barrier = pltpu.get_barrier_semaphore()

    def greet(off, carry):
        pl.semaphore_signal(barrier, inc=1, device_id={"space": lax.rem(me + off, count)}, device_id_type=MESH)
        return carry

    lax.fori_loop(1, count, greet, 0)
    pl.semaphore_wait(barrier, count - 1)

    def up_copy():
        return pltpu.make_async_remote_copy(
            src_ref=image.at[pl.ds(0, 2)], dst_ref=halo.at[1],
            send_sem=halo_send.at[0], recv_sem=halo_recv.at[1],
            device_id={"space": jnp.maximum(me - 1, 0)}, device_id_type=MESH)

    def down_copy():
        return pltpu.make_async_remote_copy(
            src_ref=image.at[pl.ds(rows - 2, 2)], dst_ref=halo.at[0],
            send_sem=halo_send.at[1], recv_sem=halo_recv.at[0],
            device_id={"space": jnp.minimum(me + 1, count - 1)}, device_id_type=MESH)

    @pl.when(me > 0)
    def _():
        up_copy().start()

    @pl.when(me < count - 1)
    def _():
        down_copy().start()

    @pl.when(me == 0)
    def _():
        halo[0] = jnp.zeros(halo.shape[1:], F32)

    @pl.when(me == count - 1)
    def _():
        halo[1] = jnp.zeros(halo.shape[1:], F32)

    total = (rows + 4) * width
    inner = rows * width
    edge = 2 * width
    zero1 = jnp.zeros((EDGE, channels), F32)
    pad1[pl.ds(0, EDGE), :] = zero1
    pad1[pl.ds(EDGE + total, EDGE), :] = zero1
    held = image[...].reshape(inner, channels)
    pad1[pl.ds(EDGE + edge, inner), :] = silu(held)
    pad2[pl.ds(0, EDGE), :] = zero1
    pad2[pl.ds(EDGE + total - edge, EDGE), :] = zero1
    zero3 = jnp.zeros((EDGE, outer), F32)
    pad3[pl.ds(0, EDGE), :] = zero3
    pad3[pl.ds(EDGE + pixels, EDGE), :] = zero3
    zero4 = jnp.zeros((EDGE, part), F32)
    pad4[pl.ds(0, EDGE), :] = zero4
    pad4[pl.ds(EDGE + pixels, EDGE), :] = zero4

    loads[0].wait()

    def split_first(t, carry):
        w1h[t], w1l[t] = split(w1[t])
        return carry

    lax.fori_loop(0, 9, split_first, 0)

    @pl.when(me > 0)
    def _():
        down_copy().wait_recv()

    @pl.when(me < count - 1)
    def _():
        up_copy().wait_recv()

    pad1[pl.ds(EDGE, edge), :] = silu(halo[0].reshape(edge, channels))
    pad1[pl.ds(EDGE + edge + inner, edge), :] = silu(halo[1].reshape(edge, channels))

    span = (rows + 2) * width
    acc = jnp.zeros((span, channels), F32)
    for dy in range(3):
        for dx in range(3):
            x = stacked(pad1, EDGE + dy * width, span, width, dx)
            both = mul(x, w1h[3 * dy + dx])
            acc = acc + (both[:span] + both[span:] + mul(x[:span], w1l[3 * dy + dx]))
    pad2[pl.ds(EDGE, span), :] = silu(acc + bias_first[...])

    @pl.when(me == 0)
    def _():
        pad2[pl.ds(EDGE, width), :] = jnp.zeros((width, channels), F32)

    @pl.when(me == count - 1)
    def _():
        pad2[pl.ds(EDGE + span - width, width), :] = jnp.zeros((width, channels), F32)

    loads[1].wait()
    acc = jnp.zeros((inner, channels), F32)
    for dy in range(3):
        for dx in range(3):
            x = stacked(pad2, EDGE + dy * width, inner, width, dx)
            wh, wl = split(w2[3 * dy + dx])
            both = mul(x, wh)
            acc = acc + (both[:inner] + both[inner:] + mul(x[:inner], wl))
    result = image[...].reshape(inner, channels) + (acc + bias_second[...])
    fine[...] = result
    fine_out[...] = result.reshape(rows, width, channels)

    per_row = width // 4
    for e in range(count):
        at = e * feature
        cell, channel = at // channels, at % channels
        ky, kx = cell // 4, cell % 4
        for p in range(local):
            row = (4 * (p // per_row) + ky) * width + 4 * (p % per_row) + kx
            patch_out[e, pl.ds(p, 1), :] = fine[pl.ds(row, 1), pl.ds(channel, feature)]

    def send_all(out, into, stage):
        def one(off, carry):
            peer = lax.rem(me + off, count)
            pltpu.make_async_remote_copy(
                src_ref=out(peer), dst_ref=into.at[me],
                send_sem=send_sem.at[stage], recv_sem=recv_sem.at[stage],
                device_id={"space": peer}, device_id_type=MESH).start()
            return carry

        lax.fori_loop(1, count, one, 0)

    def wait_all(into, sem):
        other = into.at[pl.ds(0, count - 1)]
        pltpu.make_async_copy(other, other, sem).wait()

    send_all(lambda peer: patch_out.at[peer], patch_in, 0)
    loads[2].wait()
    wph[...], wpl[...] = split(wp[...])
    patch_in[me] = patch_out[me]
    wait_all(patch_in, recv_sem.at[0])

    features = jnp.concatenate([patch_in[d] for d in range(count)], axis=0)
    high, low = split(features)
    x = jnp.concatenate([high, low], axis=0)
    chunk = 256
    for n in range(0, outer, chunk):
        cols = pl.ds(n, chunk)
        both = mul(x, wph[:, cols])
        value = both[:pixels] + both[pixels:] + mul(high, wpl[:, cols])
        for e in range(count):
            sum_out[e, :, cols] = value[local * e : local * (e + 1)]
    send_all(lambda peer: sum_out.at[peer], sum_in, 1)
    loads[3].wait()

    def split_third(t, carry):
        high, low = split(w3[t])
        w3s[t, :, pl.ds(0, part)] = high
        w3s[t, :, pl.ds(gap, part)] = low
        return carry

    lax.fori_loop(0, 9, split_third, 0)
    sum_in[me] = sum_out[me]
    wait_all(sum_in, recv_sem.at[1])

    def add_up(ref):
        value = ref[0]
        for d in range(1, count):
            value = value + ref[d]
        return value

    coarse_input = add_up(sum_in) + patch_bias[...]
    coarse_out[...] = coarse_input.reshape(coarse_out.shape)
    mine[...] = silu(coarse_input)
    send_all(lambda peer: mine, gathered, 2)
    loads[4].wait()

    def split_fourth(t, carry):
        w4h[t], w4l[t] = split(w4[t])
        return carry

    lax.fori_loop(0, 9, split_fourth, 0)
    gathered[me] = mine[...]
    wait_all(gathered, recv_sem.at[2])
    for d in range(count):
        pad3[pl.ds(EDGE + local * d, local), :] = gathered[d]

    acc = jnp.zeros((2 * pixels, 2 * gap), F32)
    for dy in range(3):
        for dx in range(3):
            x = stacked(pad3, EDGE + (dy - 1) * per_row, pixels, per_row, dx)
            acc = acc + mul(x, w3s[3 * dy + dx])
    third = acc[:pixels, :part] + acc[:pixels, gap : gap + part] + acc[pixels:, :part]
    pad4[pl.ds(EDGE, pixels), :] = silu(third + coarse_bias_first[...])

    taps = [
        stacked(pad4, EDGE + (dy - 1) * per_row, pixels, per_row, dx)
        for dy in range(3) for dx in range(3)
    ]
    for n in range(0, outer, chunk):
        cols = pl.ds(n, chunk)
        both = jnp.zeros((2 * pixels, chunk), F32)
        value = jnp.zeros((pixels, chunk), F32)
        for t in range(9):
            both = both + mul(taps[t], w4h[t, :, cols])
            value = value + mul(taps[t][:pixels], w4l[t, :, cols])
        value = value + both[:pixels] + both[pixels:]
        for e in range(count):
            last_out[e, :, cols] = value[local * e : local * (e + 1)]
    send_all(lambda peer: last_out.at[peer], last_in, 3)
    last_in[me] = last_out[me]
    wait_all(last_in, recv_sem.at[3])
    fourth = add_up(last_in) + coarse_bias_second[...]
    coarse_out[...] = coarse_out[...] + fourth.reshape(coarse_out.shape)

    @pl.when(me > 0)
    def _():
        up_copy().wait_send()

    @pl.when(me < count - 1)
    def _():
        down_copy().wait_send()

    wait_all(patch_in, send_sem.at[0])
    wait_all(sum_in, send_sem.at[1])
    wait_all(gathered, send_sem.at[2])
    wait_all(last_in, send_sem.at[3])


def body(
    image_latent,
    kernel_first,
    bias_first,
    kernel_second,
    bias_second,
    patch_kernel,
    patch_bias,
    coarse_first,
    coarse_bias_first,
    coarse_second,
    coarse_bias_second,
):
    count = lax.axis_size("space")
    rows, width, channels = image_latent.shape
    feature, outer = patch_kernel.shape
    part = coarse_first.shape[3]
    local = (rows // 4) * (width // 4)
    pixels = local * count
    gap = -(-part // 128) * 128
    total = (rows + 4) * width
    vmem = pl.BlockSpec(memory_space=pltpu.VMEM)
    hbm = pl.BlockSpec(memory_space=pl.ANY)
    dma = pltpu.SemaphoreType.DMA
    weights = (
        kernel_first.reshape(9, channels, channels),
        kernel_second.reshape(9, channels, channels),
        patch_kernel,
        coarse_first.reshape(9, outer, part),
        coarse_second.reshape(9, part, outer),
    )
    slots = (count, local, outer)
    return pl.pallas_call(
        functools.partial(kernel, count),
        out_shape=(
            jax.ShapeDtypeStruct(image_latent.shape, F32),
            jax.ShapeDtypeStruct((rows // 4, width // 4, outer), F32),
        ),
        in_specs=[vmem] * 6 + [hbm] * 5,
        out_specs=(vmem, vmem),
        scratch_shapes=[pltpu.VMEM(w.shape, F32) for w in weights]
        + [
            pltpu.VMEM((9, channels, channels), BF16),
            pltpu.VMEM((9, channels, channels), BF16),
            pltpu.VMEM((feature, outer), BF16),
            pltpu.VMEM((feature, outer), BF16),
            pltpu.VMEM((9, outer, 2 * gap), BF16),
            pltpu.VMEM((9, part, outer), BF16),
            pltpu.VMEM((9, part, outer), BF16),
            pltpu.VMEM((2, 2, width, channels), F32),
            pltpu.VMEM((total + 2 * EDGE, channels), F32),
            pltpu.VMEM((total - 2 * width + 2 * EDGE, channels), F32),
            pltpu.VMEM((rows * width, channels), F32),
            pltpu.VMEM((count, local, feature), F32),
            pltpu.VMEM((count, local, feature), F32),
            pltpu.VMEM(slots, F32),
            pltpu.VMEM(slots, F32),
            pltpu.VMEM((local, outer), F32),
            pltpu.VMEM(slots, F32),
            pltpu.VMEM((pixels + 2 * EDGE, outer), F32),
            pltpu.VMEM((pixels + 2 * EDGE, part), F32),
            pltpu.VMEM(slots, F32),
            pltpu.VMEM(slots, F32),
            dma((5,)),
            dma((2,)),
            dma((2,)),
            dma((4,)),
            dma((4,)),
        ],
        compiler_params=pltpu.CompilerParams(
            collective_id=0, has_side_effects=True, vmem_limit_bytes=60 * 1024 * 1024
        ),
    )(
        image_latent,
        bias_first[None],
        bias_second[None],
        patch_bias[None],
        coarse_bias_first[None],
        coarse_bias_second[None],
        *weights,
    )


def solution(mesh):
    placed = (
        P(("groups", "space"), None, None),
        P(),
        P(),
        P(),
        P(),
        P("space", None),
        P(),
        P(None, None, None, "space"),
        P("space"),
        P(None, None, "space", None),
        P(),
    )
    return jax.shard_map(
        body,
        mesh=mesh,
        in_specs=placed,
        out_specs=(P(("groups", "space"), None, None), P(("groups", "space"), None, None)),
        check_vma=False,
    )
```

```python
import functools

import jax
import jax.numpy as jnp
from jax import lax
from jax.experimental import pallas as pl
from jax.experimental.pallas import tpu as pltpu
from jax.sharding import PartitionSpec as P

MESH = pl.DeviceIdType.MESH
F32 = jnp.float32
BF16 = jnp.bfloat16
EDGE = 8


def split(value):
    high = value.astype(BF16)
    return high, (value - high.astype(F32)).astype(BF16)


def silu(value):
    return value / (1.0 + jnp.exp(-value))


def mul(a, b):
    return jnp.dot(a, b, preferred_element_type=F32)


def mul_rows(a, b):
    return lax.dot_general(a, b, (((1,), (1,)), ((), ())), preferred_element_type=F32)


def window(ref, first, rows, width, dx):
    value = ref[pl.ds(first + dx - 1, rows), :]
    if dx != 1:
        column = lax.broadcasted_iota(jnp.int32, value.shape, 0) % width
        value = jnp.where(column == (0 if dx == 0 else width - 1), 0.0, value)
    return value


def stacked(ref, first, rows, width, dx):
    high, low = split(window(ref, first, rows, width, dx))
    return jnp.concatenate([high, low], axis=0)


def kernel(
    count,
    image, bias_first, bias_second, patch_bias, coarse_bias_first, coarse_bias_second,
    w1_hbm, w2_hbm, wp_hbm, w3_hbm, w4_hbm,
    fine_out, coarse_out,
    w1, w2, wp, w3, w4,
    w1h, w1l, wph, wpl, w3s, w4h, w4l,
    halo, pad1, pad2, fine, patch_out, patch_in, sum_out, sum_in, mine, gathered, pad3, pad4, last_out, last_in,
    load_sem, halo_send, halo_recv, send_sem, recv_sem,
):
    me = lax.axis_index("space")
    rows, width, channels = image.shape
    local = mine.shape[0]
    pixels = local * count
    outer = wp.shape[1]
    feature = wp.shape[0]
    part = w3.shape[1]
    gap = w3s.shape[1] // 2

    loads = [
        pltpu.make_async_copy(src, dst, load_sem.at[i])
        for i, (src, dst) in enumerate(((w1_hbm, w1), (w2_hbm, w2), (wp_hbm, wp), (w3_hbm, w3), (w4_hbm, w4)))
    ]
    for load in loads:
        load.start()

    barrier = pltpu.get_barrier_semaphore()

    def greet(off, carry):
        pl.semaphore_signal(barrier, inc=1, device_id={"space": lax.rem(me + off, count)}, device_id_type=MESH)
        return carry

    lax.fori_loop(1, count, greet, 0)
    pl.semaphore_wait(barrier, count - 1)

    def up_copy():
        return pltpu.make_async_remote_copy(
            src_ref=image.at[pl.ds(0, 2)], dst_ref=halo.at[1],
            send_sem=halo_send.at[0], recv_sem=halo_recv.at[1],
            device_id={"space": jnp.maximum(me - 1, 0)}, device_id_type=MESH)

    def down_copy():
        return pltpu.make_async_remote_copy(
            src_ref=image.at[pl.ds(rows - 2, 2)], dst_ref=halo.at[0],
            send_sem=halo_send.at[1], recv_sem=halo_recv.at[0],
            device_id={"space": jnp.minimum(me + 1, count - 1)}, device_id_type=MESH)

    @pl.when(me > 0)
    def _():
        up_copy().start()

    @pl.when(me < count - 1)
    def _():
        down_copy().start()

    @pl.when(me == 0)
    def _():
        halo[0] = jnp.zeros(halo.shape[1:], F32)

    @pl.when(me == count - 1)
    def _():
        halo[1] = jnp.zeros(halo.shape[1:], F32)

    total = (rows + 4) * width
    inner = rows * width
    edge = 2 * width
    zero1 = jnp.zeros((EDGE, channels), F32)
    pad1[pl.ds(0, EDGE), :] = zero1
    pad1[pl.ds(EDGE + total, EDGE), :] = zero1
    held = image[...].reshape(inner, channels)
    pad1[pl.ds(EDGE + edge, inner), :] = silu(held)
    pad2[pl.ds(0, EDGE), :] = zero1
    pad2[pl.ds(EDGE + total - edge, EDGE), :] = zero1
    zero3 = jnp.zeros((EDGE, outer), F32)
    pad3[pl.ds(0, EDGE), :] = zero3
    pad3[pl.ds(EDGE + pixels, EDGE), :] = zero3
    zero4 = jnp.zeros((EDGE, part), F32)
    pad4[pl.ds(0, EDGE), :] = zero4
    pad4[pl.ds(EDGE + pixels, EDGE), :] = zero4

    loads[0].wait()

    def split_first(t, carry):
        w1h[t], w1l[t] = split(w1[t])
        return carry

    lax.fori_loop(0, 9, split_first, 0)

    @pl.when(me > 0)
    def _():
        down_copy().wait_recv()

    @pl.when(me < count - 1)
    def _():
        up_copy().wait_recv()

    pad1[pl.ds(EDGE, edge), :] = silu(halo[0].reshape(edge, channels))
    pad1[pl.ds(EDGE + edge + inner, edge), :] = silu(halo[1].reshape(edge, channels))

    span = (rows + 2) * width
    acc = jnp.zeros((span, channels), F32)
    for dy in range(3):
        for dx in range(3):
            x = stacked(pad1, EDGE + dy * width, span, width, dx)
            both = mul(x, w1h[3 * dy + dx])
            acc = acc + (both[:span] + both[span:] + mul(x[:span], w1l[3 * dy + dx]))
    pad2[pl.ds(EDGE, span), :] = silu(acc + bias_first[...])

    @pl.when(me == 0)
    def _():
        pad2[pl.ds(EDGE, width), :] = jnp.zeros((width, channels), F32)

    @pl.when(me == count - 1)
    def _():
        pad2[pl.ds(EDGE + span - width, width), :] = jnp.zeros((width, channels), F32)

    loads[1].wait()
    acc = jnp.zeros((inner, channels), F32)
    for dy in range(3):
        for dx in range(3):
            x = stacked(pad2, EDGE + dy * width, inner, width, dx)
            wh, wl = split(w2[3 * dy + dx])
            both = mul(x, wh)
            acc = acc + (both[:inner] + both[inner:] + mul(x[:inner], wl))
    result = image[...].reshape(inner, channels) + (acc + bias_second[...])
    fine[...] = result
    fine_out[...] = result.reshape(rows, width, channels)

    per_row = width // 4
    for e in range(count):
        at = e * feature
        cell, channel = at // channels, at % channels
        ky, kx = cell // 4, cell % 4
        for p in range(local):
            row = (4 * (p // per_row) + ky) * width + 4 * (p % per_row) + kx
            patch_out[e, pl.ds(p, 1), :] = fine[pl.ds(row, 1), pl.ds(channel, feature)]

    def send_all(out, into, stage):
        def one(off, carry):
            peer = lax.rem(me + off, count)
            pltpu.make_async_remote_copy(
                src_ref=out(peer), dst_ref=into.at[me],
                send_sem=send_sem.at[stage], recv_sem=recv_sem.at[stage],
                device_id={"space": peer}, device_id_type=MESH).start()
            return carry

        lax.fori_loop(1, count, one, 0)

    def wait_all(into, sem):
        other = into.at[pl.ds(0, count - 1)]
        pltpu.make_async_copy(other, other, sem).wait()

    send_all(lambda peer: patch_out.at[peer], patch_in, 0)
    loads[2].wait()
    wph[...], wpl[...] = split(wp[...])
    patch_in[me] = patch_out[me]
    wait_all(patch_in, recv_sem.at[0])

    features = jnp.concatenate([patch_in[d] for d in range(count)], axis=0)
    high, low = split(features)
    x = jnp.concatenate([high, low], axis=0)
    chunk = 256
    for n in range(0, outer, chunk):
        cols = pl.ds(n, chunk)
        both = mul(x, wph[:, cols])
        value = both[:pixels] + both[pixels:] + mul(high, wpl[:, cols])
        for e in range(count):
            sum_out[e, :, cols] = value[local * e : local * (e + 1)]
    send_all(lambda peer: sum_out.at[peer], sum_in, 1)
    loads[3].wait()

    def split_third(t, carry):
        high, low = split(w3[t])
        w3s[t, pl.ds(0, part), :] = high
        w3s[t, pl.ds(gap, part), :] = low
        return carry

    lax.fori_loop(0, 9, split_third, 0)
    sum_in[me] = sum_out[me]
    wait_all(sum_in, recv_sem.at[1])

    def add_up(ref):
        value = ref[0]
        for d in range(1, count):
            value = value + ref[d]
        return value

    coarse_input = add_up(sum_in) + patch_bias[...]
    coarse_out[...] = coarse_input.reshape(coarse_out.shape)
    mine[...] = silu(coarse_input)
    send_all(lambda peer: mine, gathered, 2)
    loads[4].wait()

    def split_fourth(t, carry):
        w4h[t], w4l[t] = split(w4[t])
        return carry

    lax.fori_loop(0, 9, split_fourth, 0)
    gathered[me] = mine[...]
    wait_all(gathered, recv_sem.at[2])
    for d in range(count):
        pad3[pl.ds(EDGE + local * d, local), :] = gathered[d]

    acc = jnp.zeros((2 * pixels, 2 * gap), F32)
    for dy in range(3):
        for dx in range(3):
            x = stacked(pad3, EDGE + (dy - 1) * per_row, pixels, per_row, dx)
            acc = acc + mul_rows(x, w3s[3 * dy + dx])
    third = acc[:pixels, :part] + acc[:pixels, gap : gap + part] + acc[pixels:, :part]
    pad4[pl.ds(EDGE, pixels), :] = silu(third + coarse_bias_first[...])

    taps = [
        stacked(pad4, EDGE + (dy - 1) * per_row, pixels, per_row, dx)
        for dy in range(3) for dx in range(3)
    ]
    for n in range(0, outer, chunk):
        cols = pl.ds(n, chunk)
        both = jnp.zeros((2 * pixels, chunk), F32)
        value = jnp.zeros((pixels, chunk), F32)
        for t in range(9):
            both = both + mul(taps[t], w4h[t, :, cols])
            value = value + mul(taps[t][:pixels], w4l[t, :, cols])
        value = value + both[:pixels] + both[pixels:]
        for e in range(count):
            last_out[e, :, cols] = value[local * e : local * (e + 1)]
    send_all(lambda peer: last_out.at[peer], last_in, 3)
    last_in[me] = last_out[me]
    wait_all(last_in, recv_sem.at[3])
    fourth = add_up(last_in) + coarse_bias_second[...]
    coarse_out[...] = coarse_out[...] + fourth.reshape(coarse_out.shape)

    @pl.when(me > 0)
    def _():
        up_copy().wait_send()

    @pl.when(me < count - 1)
    def _():
        down_copy().wait_send()

    wait_all(patch_in, send_sem.at[0])
    wait_all(sum_in, send_sem.at[1])
    wait_all(gathered, send_sem.at[2])
    wait_all(last_in, send_sem.at[3])


def body(
    image_latent,
    kernel_first,
    bias_first,
    kernel_second,
    bias_second,
    patch_kernel,
    patch_bias,
    coarse_first,
    coarse_bias_first,
    coarse_second,
    coarse_bias_second,
):
    count = lax.axis_size("space")
    rows, width, channels = image_latent.shape
    feature, outer = patch_kernel.shape
    part = coarse_first.shape[3]
    local = (rows // 4) * (width // 4)
    pixels = local * count
    gap = -(-part // 16) * 16
    total = (rows + 4) * width
    vmem = pl.BlockSpec(memory_space=pltpu.VMEM)
    hbm = pl.BlockSpec(memory_space=pl.ANY)
    dma = pltpu.SemaphoreType.DMA
    weights = (
        kernel_first.reshape(9, channels, channels),
        kernel_second.reshape(9, channels, channels),
        patch_kernel,
        jnp.swapaxes(coarse_first, 2, 3).reshape(9, part, outer),
        coarse_second.reshape(9, part, outer),
    )
    slots = (count, local, outer)
    return pl.pallas_call(
        functools.partial(kernel, count),
        out_shape=(
            jax.ShapeDtypeStruct(image_latent.shape, F32),
            jax.ShapeDtypeStruct((rows // 4, width // 4, outer), F32),
        ),
        in_specs=[vmem] * 6 + [hbm] * 5,
        out_specs=(vmem, vmem),
        scratch_shapes=[pltpu.VMEM(w.shape, F32) for w in weights]
        + [
            pltpu.VMEM((9, channels, channels), BF16),
            pltpu.VMEM((9, channels, channels), BF16),
            pltpu.VMEM((feature, outer), BF16),
            pltpu.VMEM((feature, outer), BF16),
            pltpu.VMEM((9, 2 * gap, outer), BF16),
            pltpu.VMEM((9, part, outer), BF16),
            pltpu.VMEM((9, part, outer), BF16),
            pltpu.VMEM((2, 2, width, channels), F32),
            pltpu.VMEM((total + 2 * EDGE, channels), F32),
            pltpu.VMEM((total - 2 * width + 2 * EDGE, channels), F32),
            pltpu.VMEM((rows * width, channels), F32),
            pltpu.VMEM((count, local, feature), F32),
            pltpu.VMEM((count, local, feature), F32),
            pltpu.VMEM(slots, F32),
            pltpu.VMEM(slots, F32),
            pltpu.VMEM((local, outer), F32),
            pltpu.VMEM(slots, F32),
            pltpu.VMEM((pixels + 2 * EDGE, outer), F32),
            pltpu.VMEM((pixels + 2 * EDGE, part), F32),
            pltpu.VMEM(slots, F32),
            pltpu.VMEM(slots, F32),
            dma((5,)),
            dma((2,)),
            dma((2,)),
            dma((4,)),
            dma((4,)),
        ],
        compiler_params=pltpu.CompilerParams(
            collective_id=0, has_side_effects=True, vmem_limit_bytes=60 * 1024 * 1024
        ),
    )(
        image_latent,
        bias_first[None],
        bias_second[None],
        patch_bias[None],
        coarse_bias_first[None],
        coarse_bias_second[None],
        *weights,
    )


def solution(mesh):
    placed = (
        P(("groups", "space"), None, None),
        P(),
        P(),
        P(),
        P(),
        P("space", None),
        P(),
        P(None, None, None, "space"),
        P("space"),
        P(None, None, "space", None),
        P(),
    )
    return jax.shard_map(
        body,
        mesh=mesh,
        in_specs=placed,
        out_specs=(P(("groups", "space"), None, None), P(("groups", "space"), None, None)),
        check_vma=False,
    )
```

```python
import functools

import jax
import jax.numpy as jnp
from jax import lax
from jax.experimental import pallas as pl
from jax.experimental.pallas import tpu as pltpu
from jax.sharding import PartitionSpec as P

MESH = pl.DeviceIdType.MESH
F32 = jnp.float32
BF16 = jnp.bfloat16
EDGE = 8


def split(value):
    high = value.astype(BF16)
    return high, (value - high.astype(F32)).astype(BF16)


def silu(value):
    return value / (1.0 + jnp.exp(-value))


def mul(a, b):
    return jnp.dot(a, b, preferred_element_type=F32)


def mul_rows(a, b):
    return lax.dot_general(a, b, (((1,), (1,)), ((), ())), preferred_element_type=F32)


def window(ref, first, rows, width, dx):
    value = ref[pl.ds(first + dx - 1, rows), :]
    if dx != 1:
        column = lax.broadcasted_iota(jnp.int32, value.shape, 0) % width
        value = jnp.where(column == (0 if dx == 0 else width - 1), 0.0, value)
    return value


def stacked(ref, first, rows, width, dx):
    high, low = split(window(ref, first, rows, width, dx))
    return jnp.concatenate([high, low], axis=0)


def kernel(
    count,
    image, bias_first, bias_second, patch_bias, coarse_bias_first, coarse_bias_second,
    w1_hbm, w2_hbm, wp_hbm, w3_hbm, w4_hbm,
    fine_out, coarse_out,
    w1, w2, wp, w3, w4,
    w1h, w1l, wph, wpl, w3s, w4h, w4l,
    halo, pad1, pad2, fine, patch_out, patch_in, sum_out, sum_in, mine, gathered, pad3, pad4, last_out, last_in,
    load_sem, halo_send, halo_recv, send_sem, recv_sem,
):
    me = lax.axis_index("space")
    rows, width, channels = image.shape
    local = mine.shape[0]
    pixels = local * count
    outer = wp.shape[1]
    feature = wp.shape[0]
    part = w3.shape[1]
    gap = w3s.shape[1] // 2

    loads = [
        pltpu.make_async_copy(src, dst, load_sem.at[i])
        for i, (src, dst) in enumerate(((w1_hbm, w1), (w2_hbm, w2), (wp_hbm, wp), (w3_hbm, w3), (w4_hbm, w4)))
    ]
    for load in loads:
        load.start()

    barrier = pltpu.get_barrier_semaphore()

    def greet(off, carry):
        pl.semaphore_signal(barrier, inc=1, device_id={"space": lax.rem(me + off, count)}, device_id_type=MESH)
        return carry

    lax.fori_loop(1, count, greet, 0)
    pl.semaphore_wait(barrier, count - 1)

    def up_copy():
        return pltpu.make_async_remote_copy(
            src_ref=image.at[pl.ds(0, 2)], dst_ref=halo.at[1],
            send_sem=halo_send.at[0], recv_sem=halo_recv.at[1],
            device_id={"space": jnp.maximum(me - 1, 0)}, device_id_type=MESH)

    def down_copy():
        return pltpu.make_async_remote_copy(
            src_ref=image.at[pl.ds(rows - 2, 2)], dst_ref=halo.at[0],
            send_sem=halo_send.at[1], recv_sem=halo_recv.at[0],
            device_id={"space": jnp.minimum(me + 1, count - 1)}, device_id_type=MESH)

    @pl.when(me > 0)
    def _():
        up_copy().start()

    @pl.when(me < count - 1)
    def _():
        down_copy().start()

    @pl.when(me == 0)
    def _():
        halo[0] = jnp.zeros(halo.shape[1:], F32)

    @pl.when(me == count - 1)
    def _():
        halo[1] = jnp.zeros(halo.shape[1:], F32)

    total = (rows + 4) * width
    inner = rows * width
    edge = 2 * width
    zero1 = jnp.zeros((EDGE, channels), F32)
    pad1[pl.ds(0, EDGE), :] = zero1
    pad1[pl.ds(EDGE + total, EDGE), :] = zero1
    held = image[...].reshape(inner, channels)
    pad1[pl.ds(EDGE + edge, inner), :] = silu(held)
    pad2[pl.ds(0, EDGE), :] = zero1
    pad2[pl.ds(EDGE + total - edge, EDGE), :] = zero1
    zero3 = jnp.zeros((EDGE, outer), F32)
    pad3[pl.ds(0, EDGE), :] = zero3
    pad3[pl.ds(EDGE + pixels, EDGE), :] = zero3
    zero4 = jnp.zeros((EDGE, part), F32)
    pad4[pl.ds(0, EDGE), :] = zero4
    pad4[pl.ds(EDGE + pixels, EDGE), :] = zero4

    loads[0].wait()

    def split_first(t, carry):
        w1h[t], w1l[t] = split(w1[t])
        return carry

    lax.fori_loop(0, 9, split_first, 0)

    @pl.when(me > 0)
    def _():
        down_copy().wait_recv()

    @pl.when(me < count - 1)
    def _():
        up_copy().wait_recv()

    pad1[pl.ds(EDGE, edge), :] = silu(halo[0].reshape(edge, channels))
    pad1[pl.ds(EDGE + edge + inner, edge), :] = silu(halo[1].reshape(edge, channels))

    span = (rows + 2) * width
    acc = jnp.zeros((span, channels), F32)
    for dy in range(3):
        for dx in range(3):
            x = stacked(pad1, EDGE + dy * width, span, width, dx)
            both = mul(x, w1h[3 * dy + dx])
            acc = acc + (both[:span] + both[span:] + mul(x[:span], w1l[3 * dy + dx]))
    pad2[pl.ds(EDGE, span), :] = silu(acc + bias_first[...])

    @pl.when(me == 0)
    def _():
        pad2[pl.ds(EDGE, width), :] = jnp.zeros((width, channels), F32)

    @pl.when(me == count - 1)
    def _():
        pad2[pl.ds(EDGE + span - width, width), :] = jnp.zeros((width, channels), F32)

    loads[1].wait()
    acc = jnp.zeros((inner, channels), F32)
    for dy in range(3):
        for dx in range(3):
            x = stacked(pad2, EDGE + dy * width, inner, width, dx)
            wh, wl = split(w2[3 * dy + dx])
            both = mul(x, wh)
            acc = acc + (both[:inner] + both[inner:] + mul(x[:inner], wl))
    result = image[...].reshape(inner, channels) + (acc + bias_second[...])
    fine[...] = result
    fine_out[...] = result.reshape(rows, width, channels)

    per_row = width // 4
    for e in range(count):
        at = e * feature
        cell, channel = at // channels, at % channels
        ky, kx = cell // 4, cell % 4
        for p in range(local):
            row = (4 * (p // per_row) + ky) * width + 4 * (p % per_row) + kx
            patch_out[e, pl.ds(p, 1), :] = fine[pl.ds(row, 1), pl.ds(channel, feature)]

    def send_all(out, into, stage, base=0):
        def one(off, carry):
            peer = lax.rem(me + off, count)
            pltpu.make_async_remote_copy(
                src_ref=out(peer), dst_ref=into.at[base + me],
                send_sem=send_sem.at[stage], recv_sem=recv_sem.at[stage],
                device_id={"space": peer}, device_id_type=MESH).start()
            return carry

        lax.fori_loop(1, count, one, 0)

    def wait_all(into, sem):
        other = into.at[pl.ds(0, into.shape[0] // count * (count - 1))]
        pltpu.make_async_copy(other, other, sem).wait()

    send_all(lambda peer: patch_out.at[peer], patch_in, 0)
    loads[2].wait()
    wph[...], wpl[...] = split(wp[...])
    patch_in[me] = patch_out[me]
    wait_all(patch_in, recv_sem.at[0])

    features = jnp.concatenate([patch_in[d] for d in range(count)], axis=0)
    high, low = split(features)
    x = jnp.concatenate([high, low], axis=0)
    chunk = sum_out.shape[2]
    for n in range(0, outer, chunk):
        cols = pl.ds(n, chunk)
        base = n // chunk * count
        both = mul(x, wph[:, cols])
        value = both[:pixels] + both[pixels:] + mul(high, wpl[:, cols])
        for e in range(count):
            sum_out[base + e] = value[local * e : local * (e + 1)]
        send_all(lambda peer: sum_out.at[base + peer], sum_in, 1, base)
    loads[3].wait()

    def split_third(t, carry):
        high, low = split(w3[t])
        w3s[t, pl.ds(0, part), :] = high
        w3s[t, pl.ds(gap, part), :] = low
        return carry

    lax.fori_loop(0, 9, split_third, 0)
    for base in range(0, sum_in.shape[0], count):
        sum_in[base + me] = sum_out[base + me]
    wait_all(sum_in, recv_sem.at[1])

    def add_up(ref):
        values = []
        for base in range(0, ref.shape[0], count):
            value = ref[base]
            for d in range(1, count):
                value = value + ref[base + d]
            values.append(value)
        return jnp.concatenate(values, axis=1)

    coarse_input = add_up(sum_in) + patch_bias[...]
    coarse_out[...] = coarse_input.reshape(coarse_out.shape)
    mine[...] = silu(coarse_input)
    send_all(lambda peer: mine, gathered, 2)
    loads[4].wait()

    def split_fourth(t, carry):
        w4h[t], w4l[t] = split(w4[t])
        return carry

    lax.fori_loop(0, 9, split_fourth, 0)
    gathered[me] = mine[...]
    wait_all(gathered, recv_sem.at[2])
    for d in range(count):
        pad3[pl.ds(EDGE + local * d, local), :] = gathered[d]

    acc = jnp.zeros((2 * pixels, 2 * gap), F32)
    for dy in range(3):
        for dx in range(3):
            x = stacked(pad3, EDGE + (dy - 1) * per_row, pixels, per_row, dx)
            acc = acc + mul_rows(x, w3s[3 * dy + dx])
    third = acc[:pixels, :part] + acc[:pixels, gap : gap + part] + acc[pixels:, :part]
    pad4[pl.ds(EDGE, pixels), :] = silu(third + coarse_bias_first[...])

    taps = [
        stacked(pad4, EDGE + (dy - 1) * per_row, pixels, per_row, dx)
        for dy in range(3) for dx in range(3)
    ]
    for n in range(0, outer, chunk):
        cols = pl.ds(n, chunk)
        base = n // chunk * count
        both = jnp.zeros((2 * pixels, chunk), F32)
        value = jnp.zeros((pixels, chunk), F32)
        for t in range(9):
            both = both + mul(taps[t], w4h[t, :, cols])
            value = value + mul(taps[t][:pixels], w4l[t, :, cols])
        value = value + both[:pixels] + both[pixels:]
        for e in range(count):
            last_out[base + e] = value[local * e : local * (e + 1)]
        send_all(lambda peer: last_out.at[base + peer], last_in, 3, base)
        last_in[base + me] = last_out[base + me]
    wait_all(last_in, recv_sem.at[3])
    fourth = add_up(last_in) + coarse_bias_second[...]
    coarse_out[...] = coarse_out[...] + fourth.reshape(coarse_out.shape)

    @pl.when(me > 0)
    def _():
        up_copy().wait_send()

    @pl.when(me < count - 1)
    def _():
        down_copy().wait_send()

    wait_all(patch_in, send_sem.at[0])
    wait_all(sum_in, send_sem.at[1])
    wait_all(gathered, send_sem.at[2])
    wait_all(last_in, send_sem.at[3])


def body(
    image_latent,
    kernel_first,
    bias_first,
    kernel_second,
    bias_second,
    patch_kernel,
    patch_bias,
    coarse_first,
    coarse_bias_first,
    coarse_second,
    coarse_bias_second,
):
    count = lax.axis_size("space")
    rows, width, channels = image_latent.shape
    feature, outer = patch_kernel.shape
    part = coarse_first.shape[3]
    local = (rows // 4) * (width // 4)
    pixels = local * count
    gap = -(-part // 16) * 16
    total = (rows + 4) * width
    vmem = pl.BlockSpec(memory_space=pltpu.VMEM)
    hbm = pl.BlockSpec(memory_space=pl.ANY)
    dma = pltpu.SemaphoreType.DMA
    weights = (
        kernel_first.reshape(9, channels, channels),
        kernel_second.reshape(9, channels, channels),
        patch_kernel,
        jnp.swapaxes(coarse_first, 2, 3).reshape(9, part, outer),
        coarse_second.reshape(9, part, outer),
    )
    slots = (count, local, outer)
    pieces = (outer // 256 * count, local, 256)
    return pl.pallas_call(
        functools.partial(kernel, count),
        out_shape=(
            jax.ShapeDtypeStruct(image_latent.shape, F32),
            jax.ShapeDtypeStruct((rows // 4, width // 4, outer), F32),
        ),
        in_specs=[vmem] * 6 + [hbm] * 5,
        out_specs=(vmem, vmem),
        scratch_shapes=[pltpu.VMEM(w.shape, F32) for w in weights]
        + [
            pltpu.VMEM((9, channels, channels), BF16),
            pltpu.VMEM((9, channels, channels), BF16),
            pltpu.VMEM((feature, outer), BF16),
            pltpu.VMEM((feature, outer), BF16),
            pltpu.VMEM((9, 2 * gap, outer), BF16),
            pltpu.VMEM((9, part, outer), BF16),
            pltpu.VMEM((9, part, outer), BF16),
            pltpu.VMEM((2, 2, width, channels), F32),
            pltpu.VMEM((total + 2 * EDGE, channels), F32),
            pltpu.VMEM((total - 2 * width + 2 * EDGE, channels), F32),
            pltpu.VMEM((rows * width, channels), F32),
            pltpu.VMEM((count, local, feature), F32),
            pltpu.VMEM((count, local, feature), F32),
            pltpu.VMEM(pieces, F32),
            pltpu.VMEM(pieces, F32),
            pltpu.VMEM((local, outer), F32),
            pltpu.VMEM(slots, F32),
            pltpu.VMEM((pixels + 2 * EDGE, outer), F32),
            pltpu.VMEM((pixels + 2 * EDGE, part), F32),
            pltpu.VMEM(pieces, F32),
            pltpu.VMEM(pieces, F32),
            dma((5,)),
            dma((2,)),
            dma((2,)),
            dma((4,)),
            dma((4,)),
        ],
        compiler_params=pltpu.CompilerParams(
            collective_id=0, has_side_effects=True, vmem_limit_bytes=60 * 1024 * 1024
        ),
    )(
        image_latent,
        bias_first[None],
        bias_second[None],
        patch_bias[None],
        coarse_bias_first[None],
        coarse_bias_second[None],
        *weights,
    )


def solution(mesh):
    placed = (
        P(("groups", "space"), None, None),
        P(),
        P(),
        P(),
        P(),
        P("space", None),
        P(),
        P(None, None, None, "space"),
        P("space"),
        P(None, None, "space", None),
        P(),
    )
    return jax.shard_map(
        body,
        mesh=mesh,
        in_specs=placed,
        out_specs=(P(("groups", "space"), None, None), P(("groups", "space"), None, None)),
        check_vma=False,
    )
```
